32 devices in a mesh: space: 16 (over z, y, core), bead: 2 (over x).
Axes of the slice: x: 2, y: 2, z: 4, core: 2. Of those that a mesh axis runs over, the one named last changes fastest.
Arguments:
- positions: float32 [8, 3, 2048], P('bead', None, 'space'), may hold values from 0 to 2
- momenta: float32 [8, 3, 2048], P('bead', None, 'space'), may hold values from -6 to 6
- masses: float32 [2048], P('space'), may hold values from 1 to 4
- features: bfloat16 [8, 2048, 128], P('bead', 'space'), may hold values from -6 to 6
- neighbours: int32 [64, 2048], P(None, 'space'), may hold values from 0 to 383
- images: int32 [64, 2048], P(None, 'space'), may hold values from 0 to 26
- face_map: int32 [2, 16, 128], P(None, 'space'), may hold values from 0 to 127, each once within a row
- w_query: bfloat16 [128, 128], replicated, may hold values from -0.5 to 0.5
- w_key: bfloat16 [128, 128], replicated, may hold values from -0.375 to 0.375
- w_value: bfloat16 [128, 128], replicated, may hold values from -2 to 2
- w_probe: bfloat16 [128, 128], replicated, may hold values from -0.5 to 0.5
- radial_rate: float32 [8], replicated, may hold values from 0.02 to 0.5
Outputs:
- new_positions: float32 [8, 3, 2048], P('bead', None, 'space')
- new_momenta: float32 [8, 3, 2048], P('bead', None, 'space')
The draws below stay inside these ranges and needn't reach their ends.
Inputs may be any that keep to these rules, and one draw needn't show every extreme that they name: `neighbours`: each entry is a row of the atom's slab's extended table: own atoms first, then the ghosts from the lower slab, then those from the upper slab. `face_map`: each row of a slab's block lists every atom of that slab once.
All inputs are finite; a program needn't handle non-finite values.
Results may differ from the reference program's by a relative error of at most 0.0025.
Values may be sent and summed in bfloat16 or wider, within the bound.
A program may use at most 64 MiB of HBM per device.

```python
import math
import jax
import jax.numpy as jnp
from jax import lax

ATOMS_DEV = 128
CHANNELS = 128
HEADS = 8
NEAR = 64
BEADS = 8
BRICKS = 16
ATOMS = 2048


def touch_ends(result, stream_key, least, largest):
    index_at = [jax.random.randint(jax.random.fold_in(stream_key, axis), (), 0, length) for axis, length in enumerate(result.shape)]
    longest = result.shape.index(max(result.shape))
    next_to = index_at[:longest] + [(index_at[longest] + 1) % result.shape[longest]] + index_at[longest + 1:]
    return result.at[tuple(index_at)].set(least).at[tuple(next_to)].set(largest)


def levels(own_key, dims, pieces, smallest, top_value):
    def one(dim, blocks):
        steps = jax.random.uniform(jax.random.fold_in(jax.random.fold_in(own_key, 6), dim), (blocks,), jnp.float32, smallest / len(pieces), top_value / len(pieces))
        return jnp.repeat(jnp.exp(steps), dims[dim] // blocks).reshape((-1,) + (1,) * (len(dims) - dim - 1))

    gain = one(*pieces[0])
    for cut in pieces[1:]:
        gain = gain * one(*cut)
    return gain


def gaussian(key, dims, scale, reach, shards=(), kind=jnp.bfloat16):
    result = scale * jax.random.normal(key, dims, jnp.float32)
    if shards:
        result = result * levels(key, dims, shards, -0.22, 0.18)
    return jnp.clip(result, -reach, reach).astype(kind)


def setup_inputs(seed: int = 0) -> dict:
    keys = jax.random.split(jax.random.key(seed), 13)
    positions = jnp.clip(2.0 * jax.random.uniform(keys[0], (BEADS, 3, ATOMS), jnp.float32) ** levels(keys[0], (BEADS, 3, ATOMS), ((0, 2), (2, 16)), -0.2, 0.2), 0.0, 2.0)
    momenta = gaussian(keys[1], (BEADS, 3, ATOMS), 1.0, 6.0, ((0, 2), (2, 16)), jnp.float32)
    masses = jnp.clip(jnp.exp(math.log(4.0) - 1.3862944 * jax.random.uniform(keys[2], (ATOMS,), jnp.float32) ** levels(keys[2], (ATOMS,), ((0, 16),), -0.2, 0.2)), 1.0, 4.0)
    features = gaussian(keys[3], (BEADS, ATOMS, CHANNELS), 1.0, 6.0, ((0, 2), (1, 16)))
    neighbours = touch_ends(jax.random.randint(keys[4], (NEAR, ATOMS), 0, 3 * ATOMS_DEV), jax.random.fold_in(keys[4], 1), 0, (3 * ATOMS_DEV) - 1).astype(jnp.int32)
    images = touch_ends(jax.random.randint(keys[5], (NEAR, ATOMS), 0, 27), jax.random.fold_in(keys[5], 1), 0, 26).astype(jnp.int32)
    face_map = jax.vmap(lambda own: jax.random.permutation(own, ATOMS_DEV))(jax.random.split(keys[6], 2 * BRICKS)).reshape((2, BRICKS, ATOMS_DEV)).astype(jnp.int32)
    w_query = gaussian(keys[7], (CHANNELS, CHANNELS), CHANNELS ** -0.5, 0.5)
    w_key = gaussian(keys[8], (CHANNELS, CHANNELS), (2 * CHANNELS) ** -0.5, 0.375)
    w_value = gaussian(keys[9], (CHANNELS, CHANNELS), (CHANNELS // 16) ** -0.5, 2.0)
    w_probe = gaussian(keys[10], (CHANNELS, CHANNELS), CHANNELS ** -0.5, 0.5)
    radial_rate = jnp.clip(jnp.exp(jax.random.uniform(keys[11], (HEADS,), jnp.float32, math.log(0.02), math.log(0.5))), 0.02, 0.5)
    return {"positions": positions, "momenta": momenta, "masses": masses, "features": features, "neighbours": neighbours, "images": images, "face_map": face_map, "w_query": w_query, "w_key": w_key, "w_value": w_value, "w_probe": w_probe, "radial_rate": radial_rate}


STIFFNESS = 1.3
BOX_LENGTH = 2.0
SCORE_CAP = 30.0

def mode_table(bead_count):
    bead_column = jnp.arange(bead_count).astype(jnp.float32)[:, None]
    mode_row = jnp.arange(bead_count).astype(jnp.float32)[None, :]
    mode_index = jnp.arange(bead_count)[None, :] + jnp.zeros((bead_count, 1), jnp.int32)
    angles = 2.0 * jnp.pi * bead_column * mode_row / bead_count
    wave_norm = jnp.sqrt(jnp.float32(2.0 / bead_count))
    flat_norm = jnp.sqrt(jnp.float32(1.0 / bead_count))
    half_count = bead_count // 2
    entries = jnp.where(mode_index < half_count, wave_norm * jnp.cos(angles), wave_norm * jnp.sin(angles))
    entries = jnp.where(mode_index == half_count, flat_norm * jnp.cos(angles), entries)
    entries = jnp.where(mode_index == 0, flat_norm + 0.0 * angles, entries)
    return entries

def frequencies(bead_count):
    mode_float = jnp.arange(bead_count).astype(jnp.float32)
    return 2.0 * STIFFNESS * jnp.sin(jnp.pi * mode_float / bead_count)

def propagate(mode_pos, mode_mom, masses, frequency):
    phase_turn = frequency[:, None, None]
    cosine_turn = jnp.cos(phase_turn)
    sine_turn = jnp.sin(phase_turn)
    safe_turn = jnp.where(phase_turn > 0, phase_turn, 1.0)
    drift_gain = jnp.where(phase_turn > 0, sine_turn / safe_turn, 1.0)
    mass_row = masses[None, None, :]
    next_pos = cosine_turn * mode_pos + drift_gain * mode_mom / mass_row
    next_mom = cosine_turn * mode_mom - mass_row * phase_turn * sine_turn * mode_pos
    return (next_pos, next_mom)

def image_offsets(images):
    offset_x = images % 3 - 1
    offset_y = images // 3 % 3 - 1
    offset_z = images // 9 - 1
    return BOX_LENGTH * jnp.stack([offset_x, offset_y, offset_z]).astype(jnp.float32)

def probe_matrices(own_features, w_query, w_key, w_value, w_probe, head_count):
    atom_count, channels = own_features.shape
    head_size = channels // head_count
    queries = jnp.dot(own_features, w_query, preferred_element_type=jnp.float32).reshape(atom_count, head_count, head_size)
    probes = jnp.dot(own_features, w_probe, preferred_element_type=jnp.float32).reshape(atom_count, head_count, head_size)
    key_heads = w_key.astype(jnp.float32).reshape(channels, head_count, head_size)
    value_heads = w_value.astype(jnp.float32).reshape(channels, head_count, head_size)
    key_probe = jnp.einsum('ahd,chd->ahc', queries, key_heads, precision=lax.Precision.HIGHEST)
    value_probe = jnp.einsum('ahd,chd->ahc', probes, value_heads, precision=lax.Precision.HIGHEST)
    return jnp.concatenate([key_probe, value_probe], axis=1).astype(jnp.bfloat16)

def attend_forces(pair_terms, offsets, radial_rate, head_size):
    head_count = radial_rate.shape[0]
    scores = pair_terms[:head_count] * head_size ** (-0.5)
    capped = SCORE_CAP * jnp.tanh(scores / SCORE_CAP)
    distance = lax.optimization_barrier(jnp.sum(offsets * offsets, axis=0))
    logits = capped - radial_rate[:, None, None] * distance[None]
    weights = jnp.exp(logits)
    attention = weights / lax.optimization_barrier(jnp.sum(weights, axis=1, keepdims=True))
    coupling = lax.optimization_barrier(jnp.sum(attention * pair_terms[head_count:], axis=0)) * (1.0 / (head_count * head_size ** 0.5))
    return lax.optimization_barrier(jnp.sum(coupling[None] * offsets, axis=1))

def brick_forces(feature_table, coordinate_table, neighbours, images, w_query, w_key, w_value, w_probe, radial_rate):
    atom_count = neighbours.shape[1]
    head_count = radial_rate.shape[0]
    head_size = feature_table.shape[1] // head_count
    probe_mats = probe_matrices(feature_table[:atom_count], w_query, w_key, w_value, w_probe, head_count)
    gathered = feature_table[neighbours]
    offsets = coordinate_table[:, neighbours] - coordinate_table[:, :atom_count][:, None, :] + image_offsets(images)
    pair_terms = jnp.einsum('kac,aec->eka', gathered.astype(jnp.float32), probe_mats.astype(jnp.float32))
    return attend_forces(pair_terms, offsets, radial_rate, head_size)

def reference(positions, momenta, masses, features, neighbours, images, face_map, w_query, w_key, w_value, w_probe, radial_rate):
    bead_count = positions.shape[0]
    brick_count = face_map.shape[1]
    atom_count = face_map.shape[2]
    channels = features.shape[2]
    near_count = neighbours.shape[0]
    feature_blocks = features.reshape(bead_count, brick_count, atom_count, channels)
    coordinate_blocks = positions.reshape(bead_count, 3, brick_count, atom_count).transpose(0, 2, 1, 3)
    from_lower = jnp.roll(face_map[1], 1, axis=0)
    from_upper = jnp.roll(face_map[0], -1, axis=0)
    lower_features = jnp.take_along_axis(jnp.roll(feature_blocks, 1, axis=1), from_lower[None, :, :, None], axis=2)
    upper_features = jnp.take_along_axis(jnp.roll(feature_blocks, -1, axis=1), from_upper[None, :, :, None], axis=2)
    lower_coords = jnp.take_along_axis(jnp.roll(coordinate_blocks, 1, axis=1), from_lower[None, :, None, :], axis=3)
    upper_coords = jnp.take_along_axis(jnp.roll(coordinate_blocks, -1, axis=1), from_upper[None, :, None, :], axis=3)
    feature_tables = jnp.concatenate([feature_blocks, lower_features, upper_features], axis=2)
    coordinate_tables = jnp.concatenate([coordinate_blocks, lower_coords, upper_coords], axis=3)
    brick_neighbours = neighbours.reshape(near_count, brick_count, atom_count).transpose(1, 0, 2)
    brick_images = images.reshape(near_count, brick_count, atom_count).transpose(1, 0, 2)

    def per_brick(items):
        return brick_forces(items[0], items[1], items[2], items[3], w_query, w_key, w_value, w_probe, radial_rate)

    def per_bead(items):
        return lax.map(per_brick, (items[0], items[1], brick_neighbours, brick_images))
    forces = lax.map(per_bead, (feature_tables, coordinate_tables))
    forces = forces.transpose(0, 2, 1, 3).reshape(bead_count, 3, brick_count * atom_count)
    kicked = momenta + forces
    transform = mode_table(bead_count)
    frequency = frequencies(bead_count)
    mode_pos = jnp.einsum('bk,bcn->kcn', transform, positions, precision=lax.Precision.HIGHEST)
    mode_mom = jnp.einsum('bk,bcn->kcn', transform, kicked, precision=lax.Precision.HIGHEST)
    next_pos, next_mom = propagate(mode_pos, mode_mom, masses, frequency)
    new_positions = jnp.einsum('bk,kcn->bcn', transform, next_pos, precision=lax.Precision.HIGHEST)
    new_momenta = jnp.einsum('bk,kcn->bcn', transform, next_mom, precision=lax.Precision.HIGHEST)
    return (new_positions, new_momenta)
```

```python
import functools
import math

import jax
import jax.numpy as jnp
import numpy as np
from jax import lax
from jax.experimental import pallas as pl
from jax.experimental.pallas import tpu as pltpu
from jax.sharding import PartitionSpec as P

STIFFNESS = 1.3
BOX_LENGTH = 2.0
SCORE_CAP = 30.0
ROWS = 8
F32 = jnp.float32
BF16 = jnp.bfloat16
NT = (((1,), (1,)), ((), ()))


def step_tables(beads):
    modes = np.arange(beads)
    turn = 2.0 * STIFFNESS * np.sin(np.pi * modes / beads)
    safe = np.where(turn > 0, turn, 1.0)
    gain = np.where(turn > 0, np.sin(turn) / safe, 1.0)
    waves = np.cos(2.0 * np.pi * np.outer(modes, modes) / beads) / beads
    return waves @ np.cos(turn), waves @ gain, waves @ (turn * np.sin(turn))


def pick(table, index):
    return jnp.take_along_axis(table, index, axis=1, mode="promise_in_bounds")


def split_two(value):
    high = value.astype(BF16)
    return jnp.concatenate([high, (value - high.astype(F32)).astype(BF16)], axis=1)


def step_kernel(
    n_space, n_bead,
    pos, mom, mass, feat, near, image, face, w_query, w_key, w_value, w_probe, rate,
    new_pos, new_mom,
    feat_halo, pos_halo, face_halo, peer_pos, peer_kick, kick,
    probes, dots_own, dots_halo, first, index_t, low_t, shift_t, own_t, offs, weights, scaled,
    feat_send, feat_recv, pos_send, pos_recv, face_send, face_recv,
    peer_send, peer_recv, kick_send, kick_recv,
):
    beads, atoms, channels = feat.shape
    near_count = near.shape[0]
    heads = rate.shape[0]
    head_size = channels // heads
    pairs = beads // 2
    terms = 2 * heads
    s = lax.axis_index("space")
    g = lax.axis_index("bead")
    upper = lax.rem(s + 1, n_space)
    lower = lax.rem(s + n_space - 1, n_space)
    peers = [lax.rem(g + r, n_bead) for r in range(1, n_bead)]

    def copy(src, dst, send, recv, target):
        return pltpu.make_async_remote_copy(
            src_ref=src, dst_ref=dst, send_sem=send, recv_sem=recv,
            device_id=target, device_id_type=pl.DeviceIdType.MESH,
        )

    barrier = pltpu.get_barrier_semaphore()
    for target in [(lower, g), (upper, g)] + [(s, q) for q in peers]:
        pl.semaphore_signal(barrier, inc=1, device_id=target, device_id_type=pl.DeviceIdType.MESH)
    pl.semaphore_wait(barrier, 2 + len(peers))

    sides = [(0, (upper, g)), (1, (lower, g))]
    face_copies = [
        copy(face.at[1 - slot], face_halo.at[slot], face_send.at[slot], face_recv.at[slot], to)
        for slot, to in sides
    ]
    pos_copies = [
        copy(pos, pos_halo.at[slot], pos_send.at[slot], pos_recv.at[slot], to) for slot, to in sides
    ]
    feat_copies = [
        [
            copy(feat.at[b], feat_halo.at[slot, b], feat_send.at[slot, b], feat_recv.at[slot, b], to)
            for slot, to in sides
        ]
        for b in range(beads)
    ]
    peer_copies = [
        copy(pos, peer_pos.at[n_bead - r - 2], peer_send.at[r], peer_recv.at[n_bead - r - 2], (s, q))
        for r, q in enumerate(peers)
    ]
    for c in face_copies + pos_copies:
        c.start()
    for both in feat_copies:
        for c in both:
            c.start()
    for c in peer_copies:
        c.start()

    near2 = jnp.concatenate([near[...], near[...]], axis=0)
    index = jnp.transpose(near2)
    index_t[...] = index
    low_t[...] = jnp.bitwise_and(index, atoms - 1)
    code = image[...]
    one = lambda test: jnp.where(test, 1, 0)
    z = one(code >= 9) + one(code >= 18)
    rest = code - 9 * z
    y = one(rest >= 3) + one(rest >= 6)
    x = rest - 3 * y
    for c, part in enumerate((x, y, z)):
        shift = BOX_LENGTH * (part.astype(F32) - 1.0)
        shift_t[c] = jnp.transpose(jnp.concatenate([shift, shift], axis=0))
    for b in range(beads):
        padded = jnp.concatenate([pos[b], jnp.zeros((5, atoms), F32)], axis=0)
        own_t[b] = jnp.transpose(padded)

    flat = feat[...].reshape(beads * atoms, channels)
    depth_head = lax.broadcasted_iota(jnp.int32, (channels, channels), 0) // head_size
    for kind, (into, out) in enumerate(((w_query, w_key), (w_probe, w_value))):
        small = split_two(jnp.dot(flat, into[...], preferred_element_type=F32))
        turned = jnp.transpose(out[...].astype(F32))
        wide = jnp.concatenate(
            [jnp.where(depth_head == h, turned, 0.0).astype(BF16) for h in range(heads)], axis=1
        )
        full = jnp.dot(small, jnp.concatenate([wide, wide], axis=0), preferred_element_type=F32)
        full = full.astype(BF16)
        for b in range(beads):
            for h in range(heads):
                probes[b, kind * heads + h] = full[
                    b * atoms : (b + 1) * atoms, h * channels : (h + 1) * channels
                ]

    half = lax.broadcasted_iota(jnp.int32, (ROWS, 2 * near_count), 1) < near_count
    chunks = atoms // ROWS

    for b in range(beads):
        dots_own[b] = lax.dot_general(
            probes[b].reshape(terms * atoms, channels), feat[b], NT, preferred_element_type=F32
        ).reshape(terms, atoms, atoms)

    def pick_own(i, carry):
        rows = pl.ds(pl.multiple_of(i * ROWS, ROWS), ROWS)
        low = low_t[rows, :]
        for p in range(pairs):
            for e in range(terms):
                a = pick(dots_own[2 * p, e, rows, :], low)
                b = pick(dots_own[2 * p + 1, e, rows, :], low)
                first[p, e, rows, :] = jnp.where(half, a, b)
        return carry

    lax.fori_loop(0, chunks, pick_own, 0)

    for c in face_copies:
        c.wait_recv()

    def remap(i, carry):
        rows = pl.ds(pl.multiple_of(i * ROWS, ROWS), ROWS)
        low = low_t[rows, :]
        full = index_t[rows, :]
        from_lower = pick(jnp.broadcast_to(face_halo[0], (ROWS, atoms)), low)
        from_upper = pick(jnp.broadcast_to(face_halo[1], (ROWS, atoms)), low)
        low_t[rows, :] = jnp.where(
            full < atoms, low, jnp.where(full < 2 * atoms, from_lower, from_upper)
        )
        return carry

    lax.fori_loop(0, chunks, remap, 0)

    for c in pos_copies:
        c.wait_recv()

    def place(i, carry):
        rows = pl.ds(pl.multiple_of(i * ROWS, ROWS), ROWS)
        low = low_t[rows, :]
        full = index_t[rows, :]
        is_own = full < atoms
        is_lower = full < 2 * atoms
        for p in range(pairs):
            for c in range(3):
                found = []
                mine = []
                for b in (2 * p, 2 * p + 1):
                    line = [
                        pick(jnp.broadcast_to(r, (ROWS, atoms)), low)
                        for r in (
                            pos[b, c : c + 1, :],
                            pos_halo[0, b, c : c + 1, :],
                            pos_halo[1, b, c : c + 1, :],
                        )
                    ]
                    found.append(jnp.where(is_own, line[0], jnp.where(is_lower, line[1], line[2])))
                    mine.append(
                        jnp.broadcast_to(own_t[b, rows, c : c + 1], (ROWS, 2 * near_count))
                    )
                gap = jnp.where(half, found[0], found[1]) - jnp.where(half, mine[0], mine[1])
                offs[p, c, rows, :] = gap + shift_t[c, rows, :]
        return carry

    lax.fori_loop(0, chunks, place, 0)

    log2e = math.log2(math.e)
    sum_row = lax.broadcasted_iota(jnp.int32, (4 * near_count, 2 * near_count), 0)
    sum_col = lax.broadcasted_iota(jnp.int32, (4 * near_count, 2 * near_count), 1)
    same_half = (jnp.bitwise_and(sum_row, near_count) > 0) == (sum_col >= near_count)
    sum_table = jnp.where(same_half, 1.0, 0.0).astype(BF16)
    pick_row = lax.broadcasted_iota(jnp.int32, (8, 2 * near_count), 0)
    pick_col = lax.broadcasted_iota(jnp.int32, (8, 2 * near_count), 1)
    in_half = (pick_row == 0) == (pick_col < near_count)
    half_table = jnp.where(in_half & (pick_row < 2), 1.0, 0.0)
    kick_copies = []

    for p in range(pairs):
        for b in (2 * p, 2 * p + 1):
            for c in feat_copies[b]:
                c.wait_recv()
            table = jnp.concatenate([feat_halo[0, b], feat_halo[1, b]], axis=0)
            dots_halo[b] = lax.dot_general(
                probes[b].reshape(terms * atoms, channels), table, NT, preferred_element_type=F32
            ).reshape(terms, atoms, 2 * atoms)

        def attend(i, carry):
            rows = pl.ds(pl.multiple_of(i * ROWS, ROWS), ROWS)
            low = low_t[rows, :]
            full = index_t[rows, :]
            is_own = full < atoms
            is_lower = full < 2 * atoms
            off = [offs[p, c, rows, :] for c in range(3)]
            distance = off[0] * off[0] + off[1] * off[1] + off[2] * off[2]

            def term(e):
                found = []
                for b in (2 * p, 2 * p + 1):
                    a = pick(dots_halo[b, e, rows, 0:atoms], low)
                    c = pick(dots_halo[b, e, rows, atoms : 2 * atoms], low)
                    found.append(jnp.where(is_lower, a, c))
                return jnp.where(is_own, first[p, e, rows, :], jnp.where(half, found[0], found[1]))

            for h in range(heads):
                capped = jnp.tanh(term(h) * (1.0 / (SCORE_CAP * head_size**0.5)))
                weight = jnp.exp2(
                    capped * (SCORE_CAP * log2e) - distance * (rate[h] * log2e)
                )
                weights[h, rows, :] = weight
                scaled[h, rows, :] = weight * term(heads + h)
            return carry

        lax.fori_loop(0, chunks, attend, 0)

        totals = jnp.dot(
            split_two(weights[...].reshape(heads * atoms, 2 * near_count)),
            sum_table,
            preferred_element_type=F32,
        ).reshape(heads, atoms, 2 * near_count)
        coupling = scaled[0] / totals[0]
        for h in range(1, heads):
            coupling = coupling + scaled[h] / totals[h]
        for c in range(3):
            force = lax.dot_general(
                half_table, coupling * offs[p, c], NT,
                precision=lax.Precision.HIGHEST, preferred_element_type=F32,
            ) * (1.0 / (heads * head_size**0.5))
            for j in range(2):
                b = 2 * p + j
                kick[b, c : c + 1, :] = mom[b, c : c + 1, :] + force[j : j + 1, :]
        for r, q in enumerate(peers):
            c = copy(
                kick.at[pl.ds(2 * p, 2)],
                peer_kick.at[n_bead - r - 2, pl.ds(2 * p, 2)],
                kick_send.at[r, p],
                kick_recv.at[n_bead - r - 2, p],
                (s, q),
            )
            c.start()
            kick_copies.append(c)

    total = beads * n_bead
    keep, gain, pull = step_tables(total)
    for c in peer_copies + kick_copies:
        c.wait_recv()
    weight = mass[...]
    inverse = 1.0 / weight
    for b in range(beads):
        kept_pos = moved = kept_mom = pulled = None
        for q in range(n_bead):
            for j in range(beads):
                where_pos = pos[j] if q == 0 else peer_pos[q - 1, j]
                where_kick = kick[j] if q == 0 else peer_kick[q - 1, j]
                d = (b - j - q * beads) % total
                parts = (
                    where_pos * float(keep[d]),
                    where_kick * float(gain[d]),
                    where_kick * float(keep[d]),
                    where_pos * float(pull[d]),
                )
                if kept_pos is None:
                    kept_pos, moved, kept_mom, pulled = parts
                else:
                    kept_pos = kept_pos + parts[0]
                    moved = moved + parts[1]
                    kept_mom = kept_mom + parts[2]
                    pulled = pulled + parts[3]
        new_pos[b] = kept_pos + moved * inverse
        new_mom[b] = kept_mom - weight * pulled

    for c in face_copies + pos_copies + peer_copies + kick_copies:
        c.wait_send()
    for both in feat_copies:
        for c in both:
            c.wait_send()


def body(
    n_space, n_bead,
    positions, momenta, masses, features, neighbours, images, face_map,
    w_query, w_key, w_value, w_probe, radial_rate,
):
    beads, atoms, channels = features.shape
    heads = radial_rate.shape[0]
    near = neighbours.shape[0]
    terms = 2 * heads
    pairs = beads // 2
    wide = 2 * near
    peers = n_bead - 1
    vmem = pl.BlockSpec(memory_space=pltpu.VMEM)
    smem = pl.BlockSpec(memory_space=pltpu.SMEM)
    dma = pltpu.SemaphoreType.DMA
    shape = jax.ShapeDtypeStruct(positions.shape, F32)
    return pl.pallas_call(
        functools.partial(step_kernel, n_space, n_bead),
        out_shape=(shape, shape),
        in_specs=[vmem] * 11 + [smem],
        out_specs=(vmem, vmem),
        scratch_shapes=[
            pltpu.VMEM((2, beads, atoms, channels), BF16),
            pltpu.VMEM((2, beads, 3, atoms), F32),
            pltpu.VMEM((2, 1, atoms), jnp.int32),
            pltpu.VMEM((peers, beads, 3, atoms), F32),
            pltpu.VMEM((peers, beads, 3, atoms), F32),
            pltpu.VMEM((beads, 3, atoms), F32),
            pltpu.VMEM((beads, terms, atoms, channels), BF16),
            pltpu.VMEM((beads, terms, atoms, atoms), F32),
            pltpu.VMEM((beads, terms, atoms, 2 * atoms), F32),
            pltpu.VMEM((pairs, terms, atoms, wide), F32),
            pltpu.VMEM((atoms, wide), jnp.int32),
            pltpu.VMEM((atoms, wide), jnp.int32),
            pltpu.VMEM((3, atoms, wide), F32),
            pltpu.VMEM((beads, atoms, 8), F32),
            pltpu.VMEM((pairs, 3, atoms, wide), F32),
            pltpu.VMEM((heads, atoms, wide), F32),
            pltpu.VMEM((heads, atoms, wide), F32),
            dma((2, beads)), dma((2, beads)), dma((2,)), dma((2,)), dma((2,)), dma((2,)),
            dma((peers,)), dma((peers,)), dma((peers, pairs)), dma((peers, pairs)),
        ],
        compiler_params=pltpu.CompilerParams(
            collective_id=0, has_side_effects=True, vmem_limit_bytes=50 * 2**20
        ),
    )(
        positions, momenta, masses.reshape(1, atoms), features, neighbours, images, face_map,
        w_query, w_key, w_value, w_probe, radial_rate,
    )


def solution(mesh):
    placed = (
        P("bead", None, "space"),
        P("bead", None, "space"),
        P("space"),
        P("bead", "space", None),
        P(None, "space"),
        P(None, "space"),
        P(None, "space", None),
        P(),
        P(),
        P(),
        P(),
        P(),
    )
    return jax.shard_map(
        functools.partial(body, mesh.shape["space"], mesh.shape["bead"]),
        mesh=mesh,
        in_specs=placed,
        out_specs=(P("bead", None, "space"), P("bead", None, "space")),
        check_vma=False,
    )
```

```python
import functools
import math

import jax
import jax.numpy as jnp
import numpy as np
from jax import lax
from jax.experimental import pallas as pl
from jax.experimental.pallas import tpu as pltpu
from jax.sharding import PartitionSpec as P

STIFFNESS = 1.3
BOX_LENGTH = 2.0
SCORE_CAP = 30.0
ROWS = 16
VMEM_GRANT = 64 * 2**20 - 2**14
F32 = jnp.float32
BF16 = jnp.bfloat16
NT = (((1,), (1,)), ((), ()))


def step_tables(beads):
    modes = np.arange(beads)
    turn = 2.0 * STIFFNESS * np.sin(np.pi * modes / beads)
    safe = np.where(turn > 0, turn, 1.0)
    gain = np.where(turn > 0, np.sin(turn) / safe, 1.0)
    waves = np.cos(2.0 * np.pi * np.outer(modes, modes) / beads) / beads
    return waves @ np.cos(turn), waves @ gain, waves @ (turn * np.sin(turn))


def pick(table, index):
    return jnp.take_along_axis(table, index, axis=1, mode="promise_in_bounds")


def split_two(value):
    high = value.astype(BF16)
    return jnp.concatenate([high, (value - high.astype(F32)).astype(BF16)], axis=1)


def step_kernel(
    n_space, n_bead,
    pos_in, mom_in, mass_in, feat_in, near_in, image_in, face_in,
    query_in, key_in, value_in, probe_in, rate_in,
    new_pos, new_mom,
    pos, mom, mass, feat, near, image, w_query, w_key, w_value, w_probe, rate, load_sem,
    feat_halo, pos_halo, face_halo, peer_pos, peer_kick, kick,
    probes, dots_own, dots_halo, first, index_t, low_t, shift_t, own_t, offs, weights, scaled,
    feat_send, feat_recv, pos_send, pos_recv, face_send, face_recv,
    peer_send, peer_recv, kick_send, kick_recv,
):
    beads, atoms, channels = feat.shape
    near_count = near.shape[0]
    heads = rate.shape[0]
    head_size = channels // heads
    pairs = beads // 2
    terms = 2 * heads
    s = lax.axis_index("space")
    g = lax.axis_index("bead")
    upper = lax.rem(s + 1, n_space)
    lower = lax.rem(s + n_space - 1, n_space)
    peers = [lax.rem(g + r, n_bead) for r in range(1, n_bead)]

    def copy(src, dst, send, recv, target):
        return pltpu.make_async_remote_copy(
            src_ref=src, dst_ref=dst, send_sem=send, recv_sem=recv,
            device_id=target, device_id_type=pl.DeviceIdType.MESH,
        )

    barrier = pltpu.get_barrier_semaphore()
    for target in [(lower, g), (upper, g)] + [(s, q) for q in peers]:
        pl.semaphore_signal(barrier, inc=1, device_id=target, device_id_type=pl.DeviceIdType.MESH)

    loads = [
        pltpu.make_async_copy(src, dst, load_sem.at[i])
        for i, (src, dst) in enumerate(
            (
                (near_in, near), (image_in, image), (pos_in, pos),
                (feat_in, feat), (query_in, w_query), (probe_in, w_probe),
                (key_in, w_key), (value_in, w_value),
                (mom_in, mom), (mass_in, mass), (rate_in, rate),
            )
        )
    ]
    for c in loads:
        c.start()

    pl.semaphore_wait(barrier, 2 + len(peers))

    sides = [(0, (upper, g)), (1, (lower, g))]
    face_copies = [
        copy(face_in.at[1 - slot], face_halo.at[slot], face_send.at[slot], face_recv.at[slot], to)
        for slot, to in sides
    ]
    pos_copies = [
        copy(pos_in, pos_halo.at[slot], pos_send.at[slot], pos_recv.at[slot], to)
        for slot, to in sides
    ]
    feat_copies = [
        [
            copy(
                feat_in.at[b],
                feat_halo.at[b, pl.ds(slot * atoms, atoms)],
                feat_send.at[slot, b],
                feat_recv.at[slot, b],
                to,
            )
            for slot, to in sides
        ]
        for b in range(beads)
    ]
    peer_copies = [
        copy(
            pos_in, peer_pos.at[n_bead - r - 2], peer_send.at[r], peer_recv.at[n_bead - r - 2],
            (s, q),
        )
        for r, q in enumerate(peers)
    ]
    for c in face_copies + pos_copies:
        c.start()
    for both in feat_copies:
        for c in both:
            c.start()
    for c in peer_copies:
        c.start()

    for c in loads[:3]:
        c.wait()
    near2 = jnp.concatenate([near[...], near[...]], axis=0)
    index = jnp.transpose(near2)
    index_t[...] = index
    low_t[...] = jnp.bitwise_and(index, atoms - 1)
    code = image[...]
    one = lambda test: jnp.where(test, 1, 0)
    z = one(code >= 9) + one(code >= 18)
    rest = code - 9 * z
    y = one(rest >= 3) + one(rest >= 6)
    x = rest - 3 * y
    for c, part in enumerate((x, y, z)):
        shift = BOX_LENGTH * (part.astype(F32) - 1.0)
        shift_t[c] = jnp.transpose(jnp.concatenate([shift, shift], axis=0))
    for c in range(3):
        padded = jnp.concatenate([pos[c], jnp.zeros((8 - beads, atoms), F32)], axis=0)
        own_t[c] = jnp.transpose(padded)

    for c in loads[3:8]:
        c.wait()
    flat = feat[...].reshape(beads * atoms, channels)
    depth_head = lax.broadcasted_iota(jnp.int32, (channels, channels), 0) // head_size
    for kind, (into, out) in enumerate(((w_query, w_key), (w_probe, w_value))):
        small = split_two(jnp.dot(flat, into[...], preferred_element_type=F32))
        turned = jnp.transpose(out[...].astype(F32))
        wide = jnp.concatenate(
            [jnp.where(depth_head == h, turned, 0.0).astype(BF16) for h in range(heads)], axis=1
        )
        full = jnp.dot(small, jnp.concatenate([wide, wide], axis=0), preferred_element_type=F32)
        full = full.astype(BF16)
        for b in range(beads):
            for h in range(heads):
                probes[b, kind * heads + h] = full[
                    b * atoms : (b + 1) * atoms, h * channels : (h + 1) * channels
                ]

    half = lax.broadcasted_iota(jnp.int32, (ROWS, 2 * near_count), 1) < near_count
    chunks = atoms // ROWS
    share = terms // chunks

    def dot_share(b, table, into, i):
        some = pl.ds(i * share, share)
        width = table.shape[0]
        into[some] = lax.dot_general(
            probes[b, some].reshape(share * atoms, channels), table[...], NT,
            preferred_element_type=F32,
        ).reshape(share, atoms, width)

    def dot_all(b, table, into):
        into[...] = lax.dot_general(
            probes[b].reshape(terms * atoms, channels), table[...], NT, preferred_element_type=F32
        ).reshape(terms, atoms, table.shape[0])

    def pick_own(p, i):
        rows = pl.ds(pl.multiple_of(i * ROWS, ROWS), ROWS)
        low = low_t[rows, :]
        for e in range(terms):
            a = pick(dots_own[2 * p][e, rows, :], low)
            b = pick(dots_own[2 * p + 1][e, rows, :], low)
            first[p][e, rows, :] = jnp.where(half, a, b)

    def place(i):
        rows = pl.ds(pl.multiple_of(i * ROWS, ROWS), ROWS)
        low = low_t[rows, :]
        full = index_t[rows, :]
        is_own = full < atoms
        is_lower = full < 2 * atoms
        spread = lambda r: jnp.broadcast_to(r, (ROWS, atoms))
        from_lower = pick(spread(face_halo[0]), low)
        from_upper = pick(spread(face_halo[1]), low)
        low = jnp.where(is_own, low, jnp.where(is_lower, from_lower, from_upper))
        low_t[rows, :] = low
        for c in range(3):
            gaps = []
            for b in range(beads):
                line = [
                    pick(spread(r), low)
                    for r in (
                        pos[c, b : b + 1, :],
                        pos_halo[0, c, b : b + 1, :],
                        pos_halo[1, c, b : b + 1, :],
                    )
                ]
                found = jnp.where(is_own, line[0], jnp.where(is_lower, line[1], line[2]))
                gaps.append(
                    found - jnp.broadcast_to(own_t[c, rows, b : b + 1], (ROWS, 2 * near_count))
                )
            shift = shift_t[c, rows, :]
            for p in range(pairs):
                offs[p, c, rows, :] = jnp.where(half, gaps[2 * p], gaps[2 * p + 1]) + shift

    def halo_share(p, i):
        for b in (2 * p, 2 * p + 1):
            dot_share(b, feat_halo.at[b], dots_halo[b], i)

    for b in (0, 1):
        dot_all(b, feat.at[b], dots_own[b])

    for p in range(pairs - 1):

        def own_step(i, carry, p=p):
            pick_own(p, i)
            for b in (2 * p + 2, 2 * p + 3):
                dot_share(b, feat.at[b], dots_own[b], i)
            return carry

        lax.fori_loop(0, chunks, own_step, 0)

    for c in face_copies + pos_copies:
        c.wait_recv()

    def place_step(i, carry):
        place(i)
        return carry

    lax.fori_loop(0, chunks, place_step, 0)

    for b in (0, 1):
        for c in feat_copies[b]:
            c.wait_recv()

    def last_own_step(i, carry):
        pick_own(pairs - 1, i)
        halo_share(0, i)
        return carry

    lax.fori_loop(0, chunks, last_own_step, 0)

    for c in loads[8:]:
        c.wait()

    log2e = math.log2(math.e)
    sum_row = lax.broadcasted_iota(jnp.int32, (4 * near_count, 2 * near_count), 0)
    sum_col = lax.broadcasted_iota(jnp.int32, (4 * near_count, 2 * near_count), 1)
    same_half = (jnp.bitwise_and(sum_row, near_count) > 0) == (sum_col >= near_count)
    sum_table = jnp.where(same_half, 1.0, 0.0).astype(BF16)
    pick_row = lax.broadcasted_iota(jnp.int32, (8, 2 * near_count), 0)
    pick_col = lax.broadcasted_iota(jnp.int32, (8, 2 * near_count), 1)
    in_half = (pick_row == 0) == (pick_col < near_count)
    half_table = jnp.where(in_half & (pick_row < 2), 1.0, 0.0)
    kick_copies = []

    for p in range(pairs):
        if p + 1 < pairs:
            for b in (2 * p + 2, 2 * p + 3):
                for c in feat_copies[b]:
                    c.wait_recv()

        def attend(i, carry, p=p):
            rows = pl.ds(pl.multiple_of(i * ROWS, ROWS), ROWS)
            low = low_t[rows, :]
            full = index_t[rows, :]
            is_own = full < atoms
            is_lower = full < 2 * atoms
            off = [offs[p, c, rows, :] for c in range(3)]
            distance = off[0] * off[0] + off[1] * off[1] + off[2] * off[2]

            def term(e):
                found = []
                for b in (2 * p, 2 * p + 1):
                    a = pick(dots_halo[b][e, rows, 0:atoms], low)
                    c = pick(dots_halo[b][e, rows, atoms : 2 * atoms], low)
                    found.append(jnp.where(is_lower, a, c))
                return jnp.where(is_own, first[p][e, rows, :], jnp.where(half, found[0], found[1]))

            for h in range(heads):
                capped = jnp.tanh(term(h) * (1.0 / (SCORE_CAP * head_size**0.5)))
                weight = jnp.exp2(
                    capped * (SCORE_CAP * log2e) - distance * (rate[h] * log2e)
                )
                weights[h, rows, :] = weight
                scaled[h, rows, :] = weight * term(heads + h)
            if p + 1 < pairs:
                halo_share(p + 1, i)
            return carry

        lax.fori_loop(0, chunks, attend, 0)

        totals = jnp.dot(
            split_two(weights[...].reshape(heads * atoms, 2 * near_count)),
            sum_table,
            preferred_element_type=F32,
        ).reshape(heads, atoms, 2 * near_count)
        coupling = scaled[0] / totals[0]
        for h in range(1, heads):
            coupling = coupling + scaled[h] / totals[h]
        for c in range(3):
            force = lax.dot_general(
                half_table, coupling * offs[p, c], NT,
                precision=lax.Precision.HIGHEST, preferred_element_type=F32,
            ) * (1.0 / (heads * head_size**0.5))
            kick[p, c] = mom[c, 2 * p : 2 * p + 2, :] + force[0:2, :]
        for r, q in enumerate(peers):
            c = copy(
                kick.at[p],
                peer_kick.at[n_bead - r - 2, p],
                kick_send.at[r, p],
                kick_recv.at[n_bead - r - 2, p],
                (s, q),
            )
            c.start()
            kick_copies.append(c)

    total = beads * n_bead
    tables = step_tables(total)
    row = lax.broadcasted_iota(jnp.int32, (beads, atoms), 0)

    def column(table, source):
        result = jnp.full((beads, atoms), float(table[(0 - source) % total]), F32)
        for b in range(1, beads):
            result = jnp.where(row == b, float(table[(b - source) % total]), result)
        return result

    for c in peer_copies:
        c.wait_recv()
    kept_pos, moved, kept_mom, pulled = [[0.0] * 3 for _ in range(4)]
    for q in range(n_bead):
        if q == 1:
            for c in kick_copies:
                c.wait_recv()
        for j in range(beads):
            keep, gain, pull = [column(t, q * beads + j) for t in tables]
            for c in range(3):
                if q == 0:
                    where_pos = pos[c, j : j + 1, :]
                    where_kick = kick[j // 2, c, j % 2 : j % 2 + 1, :]
                else:
                    where_pos = peer_pos[q - 1, c, j : j + 1, :]
                    where_kick = peer_kick[q - 1, j // 2, c, j % 2 : j % 2 + 1, :]
                where_pos = jnp.broadcast_to(where_pos, (beads, atoms))
                where_kick = jnp.broadcast_to(where_kick, (beads, atoms))
                kept_pos[c] = kept_pos[c] + where_pos * keep
                moved[c] = moved[c] + where_kick * gain
                kept_mom[c] = kept_mom[c] + where_kick * keep
                pulled[c] = pulled[c] + where_pos * pull
    weight = mass[...]
    inverse = 1.0 / weight
    for c in range(3):
        new_pos[c] = kept_pos[c] + moved[c] * inverse
        new_mom[c] = kept_mom[c] - weight * pulled[c]

    for c in face_copies + pos_copies + peer_copies + kick_copies:
        c.wait_send()
    for both in feat_copies:
        for c in both:
            c.wait_send()


def hand_out(first_in, second_in, first_out, second_out, sems):
    copies = [
        pltpu.make_async_copy(first_in, first_out, sems.at[0]),
        pltpu.make_async_copy(second_in, second_out, sems.at[1]),
    ]
    for c in copies:
        c.start()
    for c in copies:
        c.wait()


def body(
    n_space, n_bead,
    positions, momenta, masses, features, neighbours, images, face_map,
    w_query, w_key, w_value, w_probe, radial_rate,
):
    beads, atoms, channels = features.shape
    heads = radial_rate.shape[0]
    near = neighbours.shape[0]
    terms = 2 * heads
    pairs = beads // 2
    wide = 2 * near
    peers = n_bead - 1
    vmem = pl.BlockSpec(memory_space=pltpu.VMEM)
    hbm = pl.BlockSpec(memory_space=pltpu.HBM)
    dma = pltpu.SemaphoreType.DMA
    shape = jax.ShapeDtypeStruct((3, beads, atoms), F32)
    square = pltpu.VMEM((channels, channels), BF16)
    new_positions, new_momenta = pl.pallas_call(
        functools.partial(step_kernel, n_space, n_bead),
        out_shape=(shape, shape),
        in_specs=[hbm] * 12,
        out_specs=(vmem, vmem),
        scratch_shapes=[
            pltpu.VMEM((3, beads, atoms), F32),
            pltpu.VMEM((3, beads, atoms), F32),
            pltpu.VMEM((1, atoms), F32),
            pltpu.VMEM((beads, atoms, channels), BF16),
            pltpu.VMEM((near, atoms), jnp.int32),
            pltpu.VMEM((near, atoms), jnp.int32),
            square, square, square, square,
            pltpu.SMEM((heads,), F32),
            dma((11,)),
            pltpu.VMEM((beads, 2 * atoms, channels), BF16),
            pltpu.VMEM((2, 3, beads, atoms), F32),
            pltpu.VMEM((2, 1, atoms), jnp.int32),
            pltpu.VMEM((peers, 3, beads, atoms), F32),
            pltpu.VMEM((peers, pairs, 3, 2, atoms), F32),
            pltpu.VMEM((pairs, 3, 2, atoms), F32),
            pltpu.VMEM((beads, terms, atoms, channels), BF16),
            tuple(pltpu.VMEM((terms, atoms, atoms), F32) for _ in range(beads)),
            tuple(pltpu.VMEM((terms, atoms, 2 * atoms), F32) for _ in range(beads)),
            tuple(pltpu.VMEM((terms, atoms, wide), F32) for _ in range(pairs)),
            pltpu.VMEM((atoms, wide), jnp.int32),
            pltpu.VMEM((atoms, wide), jnp.int32),
            pltpu.VMEM((3, atoms, wide), F32),
            pltpu.VMEM((3, atoms, 8), F32),
            pltpu.VMEM((pairs, 3, atoms, wide), F32),
            pltpu.VMEM((heads, atoms, wide), F32),
            pltpu.VMEM((heads, atoms, wide), F32),
            dma((2, beads)), dma((2, beads)), dma((2,)), dma((2,)), dma((2,)), dma((2,)),
            dma((peers,)), dma((peers,)), dma((peers, pairs)), dma((peers, pairs)),
        ],
        compiler_params=pltpu.CompilerParams(
            collective_id=0, has_side_effects=True, vmem_limit_bytes=VMEM_GRANT
        ),
    )(
        positions.transpose(1, 0, 2), momenta.transpose(1, 0, 2), masses.reshape(1, atoms),
        features, neighbours, images, face_map, w_query, w_key, w_value, w_probe, radial_rate,
    )
    new_positions, new_momenta = pl.pallas_call(
        hand_out,
        out_shape=(shape, shape),
        in_specs=[hbm] * 2,
        out_specs=(hbm, hbm),
        scratch_shapes=[dma((2,))],
        compiler_params=pltpu.CompilerParams(vmem_limit_bytes=VMEM_GRANT),
    )(new_positions, new_momenta)
    return new_positions.transpose(1, 0, 2), new_momenta.transpose(1, 0, 2)


def solution(mesh):
    placed = (
        P("bead", None, "space"),
        P("bead", None, "space"),
        P("space"),
        P("bead", "space", None),
        P(None, "space"),
        P(None, "space"),
        P(None, "space", None),
        P(),
        P(),
        P(),
        P(),
        P(),
    )
    return jax.shard_map(
        functools.partial(body, mesh.shape["space"], mesh.shape["bead"]),
        mesh=mesh,
        in_specs=placed,
        out_specs=(P("bead", None, "space"), P("bead", None, "space")),
        check_vma=False,
    )
```

```python
import functools
import math

import jax
import jax.numpy as jnp
import numpy as np
from jax import lax
from jax.experimental import pallas as pl
from jax.experimental.pallas import tpu as pltpu
from jax.sharding import PartitionSpec as P

STIFFNESS = 1.3
BOX_LENGTH = 2.0
SCORE_CAP = 30.0
ROWS = 32
VMEM_GRANT = 64 * 2**20 - 2**14
F32 = jnp.float32
BF16 = jnp.bfloat16
NT = (((1,), (1,)), ((), ()))


def step_tables(beads):
    modes = np.arange(beads)
    turn = 2.0 * STIFFNESS * np.sin(np.pi * modes / beads)
    safe = np.where(turn > 0, turn, 1.0)
    gain = np.where(turn > 0, np.sin(turn) / safe, 1.0)
    waves = np.cos(2.0 * np.pi * np.outer(modes, modes) / beads) / beads
    return waves @ np.cos(turn), waves @ gain, waves @ (turn * np.sin(turn))


def pick(table, index):
    return jnp.take_along_axis(table, index, axis=1, mode="promise_in_bounds")


def split_two(value):
    high = value.astype(BF16)
    return jnp.concatenate([high, (value - high.astype(F32)).astype(BF16)], axis=1)


def step_kernel(
    n_space, n_bead,
    pos_in, mom_in, mass_in, feat_in, near_in, image_in, face_in,
    query_in, key_in, value_in, probe_in, rate_in,
    new_pos, new_mom,
    pos, mom, mass, feat, near, image, w_query, w_key, w_value, w_probe, rate, load_sem,
    feat_halo, pos_halo, face_halo, peer_pos, peer_kick, kick,
    probes, dots_own, dots_halo, first, index_t, low_t, shift_t, own_t, offs, weights, scaled,
    feat_send, feat_recv, pos_send, pos_recv, face_send, face_recv,
    peer_send, peer_recv, kick_send, kick_recv,
):
    beads, atoms, channels = feat.shape
    near_count = near.shape[0]
    heads = rate.shape[0]
    head_size = channels // heads
    pairs = beads // 2
    terms = 2 * heads
    s = lax.axis_index("space")
    g = lax.axis_index("bead")
    upper = lax.rem(s + 1, n_space)
    lower = lax.rem(s + n_space - 1, n_space)
    peers = [lax.rem(g + r, n_bead) for r in range(1, n_bead)]

    def copy(src, dst, send, recv, target):
        return pltpu.make_async_remote_copy(
            src_ref=src, dst_ref=dst, send_sem=send, recv_sem=recv,
            device_id=target, device_id_type=pl.DeviceIdType.MESH,
        )

    barrier = pltpu.get_barrier_semaphore()
    for target in [(lower, g), (upper, g)] + [(s, q) for q in peers]:
        pl.semaphore_signal(barrier, inc=1, device_id=target, device_id_type=pl.DeviceIdType.MESH)

    loads = [
        pltpu.make_async_copy(src, dst, load_sem.at[i])
        for i, (src, dst) in enumerate(
            (
                (near_in, near), (image_in, image), (pos_in, pos),
                (feat_in, feat), (query_in, w_query), (probe_in, w_probe),
                (key_in, w_key), (value_in, w_value),
                (mom_in, mom), (mass_in, mass), (rate_in, rate),
            )
        )
    ]
    for c in loads:
        c.start()

    pl.semaphore_wait(barrier, 2 + len(peers))

    sides = [(0, (upper, g)), (1, (lower, g))]
    face_copies = [
        copy(face_in.at[1 - slot], face_halo.at[slot], face_send.at[slot], face_recv.at[slot], to)
        for slot, to in sides
    ]
    pos_copies = [
        copy(pos_in, pos_halo.at[slot], pos_send.at[slot], pos_recv.at[slot], to)
        for slot, to in sides
    ]
    feat_copies = [
        [
            copy(
                feat_in.at[b],
                feat_halo.at[b, pl.ds(slot * atoms, atoms)],
                feat_send.at[slot, b],
                feat_recv.at[slot, b],
                to,
            )
            for slot, to in sides
        ]
        for b in range(beads)
    ]
    peer_copies = [
        copy(
            pos_in, peer_pos.at[n_bead - r - 2], peer_send.at[r], peer_recv.at[n_bead - r - 2],
            (s, q),
        )
        for r, q in enumerate(peers)
    ]
    for c in face_copies + pos_copies:
        c.start()
    for both in feat_copies:
        for c in both:
            c.start()
    for c in peer_copies:
        c.start()

    for c in loads[:3]:
        c.wait()
    near2 = jnp.concatenate([near[...], near[...]], axis=0)
    index = jnp.transpose(near2)
    index_t[...] = index
    low_t[...] = jnp.bitwise_and(index, atoms - 1)
    code = image[...]
    one = lambda test: jnp.where(test, 1, 0)
    z = one(code >= 9) + one(code >= 18)
    rest = code - 9 * z
    y = one(rest >= 3) + one(rest >= 6)
    x = rest - 3 * y
    for c, part in enumerate((x, y, z)):
        shift = BOX_LENGTH * (part.astype(F32) - 1.0)
        shift_t[c] = jnp.transpose(jnp.concatenate([shift, shift], axis=0))
    for c in range(3):
        padded = jnp.concatenate([pos[c], jnp.zeros((8 - beads, atoms), F32)], axis=0)
        own_t[c] = jnp.transpose(padded)

    for c in loads[3:8]:
        c.wait()
    flat = feat[...].reshape(beads * atoms, channels)
    depth_head = lax.broadcasted_iota(jnp.int32, (channels, channels), 0) // head_size
    for kind, (into, out) in enumerate(((w_query, w_key), (w_probe, w_value))):
        small = split_two(jnp.dot(flat, into[...], preferred_element_type=F32))
        turned = jnp.transpose(out[...].astype(F32))
        wide = jnp.concatenate(
            [jnp.where(depth_head == h, turned, 0.0).astype(BF16) for h in range(heads)], axis=1
        )
        full = jnp.dot(small, jnp.concatenate([wide, wide], axis=0), preferred_element_type=F32)
        full = full.astype(BF16)
        for b in range(beads):
            for h in range(heads):
                probes[b, kind * heads + h] = full[
                    b * atoms : (b + 1) * atoms, h * channels : (h + 1) * channels
                ]

    half = lax.broadcasted_iota(jnp.int32, (ROWS, 2 * near_count), 1) < near_count
    chunks = atoms // ROWS
    share = terms // chunks

    def dot_share(b, table, into, i):
        some = pl.ds(i * share, share)
        width = table.shape[0]
        into[some] = lax.dot_general(
            probes[b, some].reshape(share * atoms, channels), table[...], NT,
            preferred_element_type=F32,
        ).reshape(share, atoms, width)

    def dot_all(b, table, into):
        into[...] = lax.dot_general(
            probes[b].reshape(terms * atoms, channels), table[...], NT, preferred_element_type=F32
        ).reshape(terms, atoms, table.shape[0])

    def pick_own(p, i):
        rows = pl.ds(pl.multiple_of(i * ROWS, ROWS), ROWS)
        low = low_t[rows, :]
        for e in range(terms):
            a = pick(dots_own[2 * p][e, rows, :], low)
            b = pick(dots_own[2 * p + 1][e, rows, :], low)
            first[p][e, rows, :] = jnp.where(half, a, b)

    def place(i):
        rows = pl.ds(pl.multiple_of(i * ROWS, ROWS), ROWS)
        low = low_t[rows, :]
        full = index_t[rows, :]
        is_own = full < atoms
        is_lower = full < 2 * atoms
        spread = lambda r: jnp.broadcast_to(r, (ROWS, atoms))
        from_lower = pick(spread(face_halo[0]), low)
        from_upper = pick(spread(face_halo[1]), low)
        low = jnp.where(is_own, low, jnp.where(is_lower, from_lower, from_upper))
        low_t[rows, :] = low
        for c in range(3):
            gaps = []
            for b in range(beads):
                line = [
                    pick(spread(r), low)
                    for r in (
                        pos[c, b : b + 1, :],
                        pos_halo[0, c, b : b + 1, :],
                        pos_halo[1, c, b : b + 1, :],
                    )
                ]
                found = jnp.where(is_own, line[0], jnp.where(is_lower, line[1], line[2]))
                gaps.append(
                    found - jnp.broadcast_to(own_t[c, rows, b : b + 1], (ROWS, 2 * near_count))
                )
            shift = shift_t[c, rows, :]
            for p in range(pairs):
                offs[p, c, rows, :] = jnp.where(half, gaps[2 * p], gaps[2 * p + 1]) + shift

    def halo_share(p, i):
        for b in (2 * p, 2 * p + 1):
            dot_share(b, feat_halo.at[b], dots_halo[b], i)

    for b in (0, 1):
        dot_all(b, feat.at[b], dots_own[b])

    for p in range(pairs - 1):

        def own_step(i, carry, p=p):
            pick_own(p, i)
            for b in (2 * p + 2, 2 * p + 3):
                dot_share(b, feat.at[b], dots_own[b], i)
            return carry

        lax.fori_loop(0, chunks, own_step, 0)

    for c in face_copies + pos_copies:
        c.wait_recv()
    for b in (0, 1):
        for c in feat_copies[b]:
            c.wait_recv()

    def last_own_step(i, carry):
        pick_own(pairs - 1, i)
        place(i)
        halo_share(0, i)
        return carry

    lax.fori_loop(0, chunks, last_own_step, 0)

    for c in loads[8:]:
        c.wait()

    log2e = math.log2(math.e)
    sum_row = lax.broadcasted_iota(jnp.int32, (4 * near_count, 2 * near_count), 0)
    sum_col = lax.broadcasted_iota(jnp.int32, (4 * near_count, 2 * near_count), 1)
    same_half = (jnp.bitwise_and(sum_row, near_count) > 0) == (sum_col >= near_count)
    sum_table = jnp.where(same_half, 1.0, 0.0).astype(BF16)
    pick_row = lax.broadcasted_iota(jnp.int32, (8, 2 * near_count), 0)
    pick_col = lax.broadcasted_iota(jnp.int32, (8, 2 * near_count), 1)
    in_half = (pick_row == 0) == (pick_col < near_count)
    half_table = jnp.where(in_half & (pick_row < 2), 1.0, 0.0)
    kick_copies = []

    for p in range(pairs):
        if p + 1 < pairs:
            for b in (2 * p + 2, 2 * p + 3):
                for c in feat_copies[b]:
                    c.wait_recv()

        def attend(i, carry, p=p):
            rows = pl.ds(pl.multiple_of(i * ROWS, ROWS), ROWS)
            low = low_t[rows, :]
            full = index_t[rows, :]
            is_own = full < atoms
            is_lower = full < 2 * atoms
            off = [offs[p, c, rows, :] for c in range(3)]
            distance = off[0] * off[0] + off[1] * off[1] + off[2] * off[2]

            def term(e):
                found = []
                for b in (2 * p, 2 * p + 1):
                    a = pick(dots_halo[b][e, rows, 0:atoms], low)
                    c = pick(dots_halo[b][e, rows, atoms : 2 * atoms], low)
                    found.append(jnp.where(is_lower, a, c))
                return jnp.where(is_own, first[p][e, rows, :], jnp.where(half, found[0], found[1]))

            for h in range(heads):
                capped = jnp.tanh(term(h) * (1.0 / (SCORE_CAP * head_size**0.5)))
                weight = jnp.exp2(
                    capped * (SCORE_CAP * log2e) - distance * (rate[h] * log2e)
                )
                weights[h, rows, :] = weight
                scaled[h, rows, :] = weight * term(heads + h)
            if p + 1 < pairs:
                halo_share(p + 1, i)
            return carry

        lax.fori_loop(0, chunks, attend, 0)

        totals = jnp.dot(
            split_two(weights[...].reshape(heads * atoms, 2 * near_count)),
            sum_table,
            preferred_element_type=F32,
        ).reshape(heads, atoms, 2 * near_count)
        coupling = scaled[0] / totals[0]
        for h in range(1, heads):
            coupling = coupling + scaled[h] / totals[h]
        for c in range(3):
            force = lax.dot_general(
                half_table, coupling * offs[p, c], NT,
                precision=lax.Precision.HIGHEST, preferred_element_type=F32,
            ) * (1.0 / (heads * head_size**0.5))
            kick[p, c] = mom[c, 2 * p : 2 * p + 2, :] + force[0:2, :]
        for r, q in enumerate(peers):
            c = copy(
                kick.at[p],
                peer_kick.at[n_bead - r - 2, p],
                kick_send.at[r, p],
                kick_recv.at[n_bead - r - 2, p],
                (s, q),
            )
            c.start()
            kick_copies.append(c)

    total = beads * n_bead
    tables = step_tables(total)
    row = lax.broadcasted_iota(jnp.int32, (beads, atoms), 0)

    def column(table, source):
        result = jnp.full((beads, atoms), float(table[(0 - source) % total]), F32)
        for b in range(1, beads):
            result = jnp.where(row == b, float(table[(b - source) % total]), result)
        return result

    for c in peer_copies:
        c.wait_recv()
    kept_pos, moved, kept_mom, pulled = [[0.0] * 3 for _ in range(4)]
    for q in range(n_bead):
        if q == 1:
            for c in kick_copies:
                c.wait_recv()
        for j in range(beads):
            keep, gain, pull = [column(t, q * beads + j) for t in tables]
            for c in range(3):
                if q == 0:
                    where_pos = pos[c, j : j + 1, :]
                    where_kick = kick[j // 2, c, j % 2 : j % 2 + 1, :]
                else:
                    where_pos = peer_pos[q - 1, c, j : j + 1, :]
                    where_kick = peer_kick[q - 1, j // 2, c, j % 2 : j % 2 + 1, :]
                where_pos = jnp.broadcast_to(where_pos, (beads, atoms))
                where_kick = jnp.broadcast_to(where_kick, (beads, atoms))
                kept_pos[c] = kept_pos[c] + where_pos * keep
                moved[c] = moved[c] + where_kick * gain
                kept_mom[c] = kept_mom[c] + where_kick * keep
                pulled[c] = pulled[c] + where_pos * pull
    weight = mass[...]
    inverse = 1.0 / weight
    for c in range(3):
        new_pos[c] = kept_pos[c] + moved[c] * inverse
        new_mom[c] = kept_mom[c] - weight * pulled[c]

    for c in face_copies + pos_copies + peer_copies + kick_copies:
        c.wait_send()
    for both in feat_copies:
        for c in both:
            c.wait_send()


def hand_out(first_in, second_in, first_out, second_out, sems):
    copies = [
        pltpu.make_async_copy(first_in, first_out, sems.at[0]),
        pltpu.make_async_copy(second_in, second_out, sems.at[1]),
    ]
    for c in copies:
        c.start()
    for c in copies:
        c.wait()


def body(
    n_space, n_bead,
    positions, momenta, masses, features, neighbours, images, face_map,
    w_query, w_key, w_value, w_probe, radial_rate,
):
    beads, atoms, channels = features.shape
    heads = radial_rate.shape[0]
    near = neighbours.shape[0]
    terms = 2 * heads
    pairs = beads // 2
    wide = 2 * near
    peers = n_bead - 1
    vmem = pl.BlockSpec(memory_space=pltpu.VMEM)
    hbm = pl.BlockSpec(memory_space=pltpu.HBM)
    dma = pltpu.SemaphoreType.DMA
    shape = jax.ShapeDtypeStruct((3, beads, atoms), F32)
    square = pltpu.VMEM((channels, channels), BF16)
    new_positions, new_momenta = pl.pallas_call(
        functools.partial(step_kernel, n_space, n_bead),
        out_shape=(shape, shape),
        in_specs=[hbm] * 12,
        out_specs=(vmem, vmem),
        scratch_shapes=[
            pltpu.VMEM((3, beads, atoms), F32),
            pltpu.VMEM((3, beads, atoms), F32),
            pltpu.VMEM((1, atoms), F32),
            pltpu.VMEM((beads, atoms, channels), BF16),
            pltpu.VMEM((near, atoms), jnp.int32),
            pltpu.VMEM((near, atoms), jnp.int32),
            square, square, square, square,
            pltpu.SMEM((heads,), F32),
            dma((11,)),
            pltpu.VMEM((beads, 2 * atoms, channels), BF16),
            pltpu.VMEM((2, 3, beads, atoms), F32),
            pltpu.VMEM((2, 1, atoms), jnp.int32),
            pltpu.VMEM((peers, 3, beads, atoms), F32),
            pltpu.VMEM((peers, pairs, 3, 2, atoms), F32),
            pltpu.VMEM((pairs, 3, 2, atoms), F32),
            pltpu.VMEM((beads, terms, atoms, channels), BF16),
            tuple(pltpu.VMEM((terms, atoms, atoms), F32) for _ in range(beads)),
            tuple(pltpu.VMEM((terms, atoms, 2 * atoms), F32) for _ in range(beads)),
            tuple(pltpu.VMEM((terms, atoms, wide), F32) for _ in range(pairs)),
            pltpu.VMEM((atoms, wide), jnp.int32),
            pltpu.VMEM((atoms, wide), jnp.int32),
            pltpu.VMEM((3, atoms, wide), F32),
            pltpu.VMEM((3, atoms, 8), F32),
            pltpu.VMEM((pairs, 3, atoms, wide), F32),
            pltpu.VMEM((heads, atoms, wide), F32),
            pltpu.VMEM((heads, atoms, wide), F32),
            dma((2, beads)), dma((2, beads)), dma((2,)), dma((2,)), dma((2,)), dma((2,)),
            dma((peers,)), dma((peers,)), dma((peers, pairs)), dma((peers, pairs)),
        ],
        compiler_params=pltpu.CompilerParams(
            collective_id=0, has_side_effects=True, vmem_limit_bytes=VMEM_GRANT
        ),
    )(
        positions.transpose(1, 0, 2), momenta.transpose(1, 0, 2), masses.reshape(1, atoms),
        features, neighbours, images, face_map, w_query, w_key, w_value, w_probe, radial_rate,
    )
    new_positions, new_momenta = pl.pallas_call(
        hand_out,
        out_shape=(shape, shape),
        in_specs=[vmem] * 2,
        out_specs=(hbm, hbm),
        scratch_shapes=[dma((2,))],
        compiler_params=pltpu.CompilerParams(vmem_limit_bytes=VMEM_GRANT),
    )(new_positions, new_momenta)
    return new_positions.transpose(1, 0, 2), new_momenta.transpose(1, 0, 2)


def solution(mesh):
    placed = (
        P("bead", None, "space"),
        P("bead", None, "space"),
        P("space"),
        P("bead", "space", None),
        P(None, "space"),
        P(None, "space"),
        P(None, "space", None),
        P(),
        P(),
        P(),
        P(),
        P(),
    )
    return jax.shard_map(
        functools.partial(body, mesh.shape["space"], mesh.shape["bead"]),
        mesh=mesh,
        in_specs=placed,
        out_specs=(P("bead", None, "space"), P("bead", None, "space")),
        check_vma=False,
    )
```

```python
import functools
import math

import jax
import jax.numpy as jnp
import numpy as np
from jax import lax
from jax.experimental import pallas as pl
from jax.experimental.pallas import tpu as pltpu
from jax.sharding import PartitionSpec as P

STIFFNESS = 1.3
BOX_LENGTH = 2.0
SCORE_CAP = 30.0
ROWS = 8
BLOCKS = 2
VMEM_GRANT = 64 * 2**20 - 2**14
F32 = jnp.float32
BF16 = jnp.bfloat16
NT = (((1,), (1,)), ((), ()))


def step_tables(beads):
    modes = np.arange(beads)
    turn = 2.0 * STIFFNESS * np.sin(np.pi * modes / beads)
    safe = np.where(turn > 0, turn, 1.0)
    gain = np.where(turn > 0, np.sin(turn) / safe, 1.0)
    waves = np.cos(2.0 * np.pi * np.outer(modes, modes) / beads) / beads
    return waves @ np.cos(turn), waves @ gain, waves @ (turn * np.sin(turn))


def pick(table, index):
    return jnp.take_along_axis(table, index, axis=1, mode="promise_in_bounds")


def split_two(value):
    high = value.astype(BF16)
    return jnp.concatenate([high, (value - high.astype(F32)).astype(BF16)], axis=1)


def step_kernel(
    n_space, n_bead,
    pos_in, mom_in, mass_in, feat_in, near_in, image_in, face_in,
    query_in, key_in, value_in, probe_in, rate_in,
    new_pos, new_mom,
    pos, mom, mass, feat, near, image, w_query, w_key, w_value, w_probe, rate, load_sem,
    feat_halo, pos_halo, face_halo, peer_pos, peer_kick, kick,
    probes, dots_own, dots_halo, first, index_t, low_t, shift_t, own_t, offs, weights, scaled,
    feat_send, feat_recv, pos_send, pos_recv, face_send, face_recv,
    peer_send, peer_recv, kick_send, kick_recv,
):
    beads, atoms, channels = feat.shape
    near_count = near.shape[0]
    heads = rate.shape[0]
    head_size = channels // heads
    pairs = beads // 2
    terms = 2 * heads
    s = lax.axis_index("space")
    g = lax.axis_index("bead")
    upper = lax.rem(s + 1, n_space)
    lower = lax.rem(s + n_space - 1, n_space)
    peers = [lax.rem(g + r, n_bead) for r in range(1, n_bead)]

    def copy(src, dst, send, recv, target):
        return pltpu.make_async_remote_copy(
            src_ref=src, dst_ref=dst, send_sem=send, recv_sem=recv,
            device_id=target, device_id_type=pl.DeviceIdType.MESH,
        )

    barrier = pltpu.get_barrier_semaphore()
    for target in [(lower, g), (upper, g)] + [(s, q) for q in peers]:
        pl.semaphore_signal(barrier, inc=1, device_id=target, device_id_type=pl.DeviceIdType.MESH)

    loads = [
        pltpu.make_async_copy(src, dst, load_sem.at[i])
        for i, (src, dst) in enumerate(
            (
                (near_in, near), (image_in, image), (pos_in, pos),
                (feat_in, feat), (query_in, w_query), (probe_in, w_probe),
                (key_in, w_key), (value_in, w_value),
                (mom_in, mom), (mass_in, mass), (rate_in, rate),
            )
        )
    ]
    for c in loads:
        c.start()

    pl.semaphore_wait(barrier, 2 + len(peers))

    sides = [(0, (upper, g)), (1, (lower, g))]
    face_copies = [
        copy(face_in.at[1 - slot], face_halo.at[slot], face_send.at[slot], face_recv.at[slot], to)
        for slot, to in sides
    ]
    pos_copies = [
        copy(pos_in, pos_halo.at[slot], pos_send.at[slot], pos_recv.at[slot], to)
        for slot, to in sides
    ]
    feat_copies = [
        [
            copy(
                feat_in.at[b],
                feat_halo.at[b, pl.ds(slot * atoms, atoms)],
                feat_send.at[slot, b],
                feat_recv.at[slot, b],
                to,
            )
            for slot, to in sides
        ]
        for b in range(beads)
    ]
    peer_copies = [
        copy(
            pos_in, peer_pos.at[n_bead - r - 2], peer_send.at[r], peer_recv.at[n_bead - r - 2],
            (s, q),
        )
        for r, q in enumerate(peers)
    ]
    for c in face_copies + pos_copies:
        c.start()
    for both in feat_copies:
        for c in both:
            c.start()
    for c in peer_copies:
        c.start()

    for c in loads[:3]:
        c.wait()
    near2 = jnp.concatenate([near[...], near[...]], axis=0)
    index = jnp.transpose(near2)
    index_t[...] = index
    low_t[...] = jnp.bitwise_and(index, atoms - 1)
    code = image[...]
    one = lambda test: jnp.where(test, 1, 0)
    z = one(code >= 9) + one(code >= 18)
    rest = code - 9 * z
    y = one(rest >= 3) + one(rest >= 6)
    x = rest - 3 * y
    for c, part in enumerate((x, y, z)):
        shift = BOX_LENGTH * (part.astype(F32) - 1.0)
        shift_t[c] = jnp.transpose(jnp.concatenate([shift, shift], axis=0))
    for c in range(3):
        padded = jnp.concatenate([pos[c], jnp.zeros((8 - beads, atoms), F32)], axis=0)
        own_t[c] = jnp.transpose(padded)

    for c in loads[3:8]:
        c.wait()
    flat = feat[...].reshape(beads * atoms, channels)
    depth_head = lax.broadcasted_iota(jnp.int32, (channels, channels), 0) // head_size
    for kind, (into, out) in enumerate(((w_query, w_key), (w_probe, w_value))):
        small = split_two(jnp.dot(flat, into[...], preferred_element_type=F32))
        turned = jnp.transpose(out[...].astype(F32))
        wide = jnp.concatenate(
            [jnp.where(depth_head == h, turned, 0.0).astype(BF16) for h in range(heads)], axis=1
        )
        full = jnp.dot(small, jnp.concatenate([wide, wide], axis=0), preferred_element_type=F32)
        full = full.astype(BF16)
        for b in range(beads):
            for h in range(heads):
                probes[b, kind * heads + h] = full[
                    b * atoms : (b + 1) * atoms, h * channels : (h + 1) * channels
                ]

    half = lax.broadcasted_iota(jnp.int32, (ROWS, 2 * near_count), 1) < near_count
    chunks = atoms // (ROWS * BLOCKS)
    share = terms // chunks

    def dot_share(b, table, into, i):
        some = pl.ds(i * share, share)
        width = table.shape[0]
        into[some] = lax.dot_general(
            probes[b, some].reshape(share * atoms, channels), table[...], NT,
            preferred_element_type=F32,
        ).reshape(share, atoms, width)

    def dot_all(b, table, into):
        into[...] = lax.dot_general(
            probes[b].reshape(terms * atoms, channels), table[...], NT, preferred_element_type=F32
        ).reshape(terms, atoms, table.shape[0])

    def pick_own(p, i):
        rows = pl.ds(pl.multiple_of(i * ROWS, ROWS), ROWS)
        low = low_t[rows, :]
        for e in range(terms):
            a = pick(dots_own[2 * p][e, rows, :], low)
            b = pick(dots_own[2 * p + 1][e, rows, :], low)
            first[p][e, rows, :] = jnp.where(half, a, b)

    def place(i):
        rows = pl.ds(pl.multiple_of(i * ROWS, ROWS), ROWS)
        low = low_t[rows, :]
        full = index_t[rows, :]
        is_own = full < atoms
        is_lower = full < 2 * atoms
        spread = lambda r: jnp.broadcast_to(r, (ROWS, atoms))
        from_lower = pick(spread(face_halo[0]), low)
        from_upper = pick(spread(face_halo[1]), low)
        low = jnp.where(is_own, low, jnp.where(is_lower, from_lower, from_upper))
        low_t[rows, :] = low
        for c in range(3):
            gaps = []
            for b in range(beads):
                line = [
                    pick(spread(r), low)
                    for r in (
                        pos[c, b : b + 1, :],
                        pos_halo[0, c, b : b + 1, :],
                        pos_halo[1, c, b : b + 1, :],
                    )
                ]
                found = jnp.where(is_own, line[0], jnp.where(is_lower, line[1], line[2]))
                gaps.append(
                    found - jnp.broadcast_to(own_t[c, rows, b : b + 1], (ROWS, 2 * near_count))
                )
            shift = shift_t[c, rows, :]
            for p in range(pairs):
                offs[p, c, rows, :] = jnp.where(half, gaps[2 * p], gaps[2 * p + 1]) + shift

    def halo_share(p, i):
        for b in (2 * p, 2 * p + 1):
            dot_share(b, feat_halo.at[b], dots_halo[b], i)

    for b in (0, 1):
        dot_all(b, feat.at[b], dots_own[b])

    for p in range(pairs - 1):

        def own_step(i, carry, p=p):
            for b in (2 * p + 2, 2 * p + 3):
                dot_share(b, feat.at[b], dots_own[b], i)
            for k in range(BLOCKS):
                pick_own(p, i * BLOCKS + k)
            return carry

        lax.fori_loop(0, chunks, own_step, 0)

    for c in face_copies + pos_copies:
        c.wait_recv()

    def place_step(i, carry):
        for k in range(BLOCKS):
            place(i * BLOCKS + k)
        return carry

    lax.fori_loop(0, chunks, place_step, 0)

    for b in (0, 1):
        for c in feat_copies[b]:
            c.wait_recv()

    def last_own_step(i, carry):
        halo_share(0, i)
        for k in range(BLOCKS):
            pick_own(pairs - 1, i * BLOCKS + k)
        return carry

    lax.fori_loop(0, chunks, last_own_step, 0)

    for c in loads[8:]:
        c.wait()

    log2e = math.log2(math.e)
    sum_row = lax.broadcasted_iota(jnp.int32, (4 * near_count, 2 * near_count), 0)
    sum_col = lax.broadcasted_iota(jnp.int32, (4 * near_count, 2 * near_count), 1)
    same_half = (jnp.bitwise_and(sum_row, near_count) > 0) == (sum_col >= near_count)
    sum_table = jnp.where(same_half, 1.0, 0.0).astype(BF16)
    pick_row = lax.broadcasted_iota(jnp.int32, (8, 2 * near_count), 0)
    pick_col = lax.broadcasted_iota(jnp.int32, (8, 2 * near_count), 1)
    in_half = (pick_row == 0) == (pick_col < near_count)
    half_table = jnp.where(in_half & (pick_row < 2), 1.0, 0.0)
    kick_copies = []

    for p in range(pairs):
        if p + 1 < pairs:
            for b in (2 * p + 2, 2 * p + 3):
                for c in feat_copies[b]:
                    c.wait_recv()

        def attend(i, p=p):
            rows = pl.ds(pl.multiple_of(i * ROWS, ROWS), ROWS)
            low = low_t[rows, :]
            full = index_t[rows, :]
            is_own = full < atoms
            is_lower = full < 2 * atoms
            off = [offs[p, c, rows, :] for c in range(3)]
            distance = off[0] * off[0] + off[1] * off[1] + off[2] * off[2]

            def term(e):
                found = []
                for b in (2 * p, 2 * p + 1):
                    a = pick(dots_halo[b][e, rows, 0:atoms], low)
                    c = pick(dots_halo[b][e, rows, atoms : 2 * atoms], low)
                    found.append(jnp.where(is_lower, a, c))
                return jnp.where(is_own, first[p][e, rows, :], jnp.where(half, found[0], found[1]))

            for h in range(heads):
                capped = jnp.tanh(term(h) * (1.0 / (SCORE_CAP * head_size**0.5)))
                weight = jnp.exp2(
                    capped * (SCORE_CAP * log2e) - distance * (rate[h] * log2e)
                )
                weights[h, rows, :] = weight
                scaled[h, rows, :] = weight * term(heads + h)

        def attend_step(i, carry, p=p, attend=attend):
            if p + 1 < pairs:
                halo_share(p + 1, i)
            for k in range(BLOCKS):
                attend(i * BLOCKS + k)
            return carry

        lax.fori_loop(0, chunks, attend_step, 0)

        totals = jnp.dot(
            split_two(weights[...].reshape(heads * atoms, 2 * near_count)),
            sum_table,
            preferred_element_type=F32,
        ).reshape(heads, atoms, 2 * near_count)
        coupling = scaled[0] / totals[0]
        for h in range(1, heads):
            coupling = coupling + scaled[h] / totals[h]
        for c in range(3):
            force = lax.dot_general(
                half_table, coupling * offs[p, c], NT,
                precision=lax.Precision.HIGHEST, preferred_element_type=F32,
            ) * (1.0 / (heads * head_size**0.5))
            kick[p, c] = mom[c, 2 * p : 2 * p + 2, :] + force[0:2, :]
        for r, q in enumerate(peers):
            c = copy(
                kick.at[p],
                peer_kick.at[n_bead - r - 2, p],
                kick_send.at[r, p],
                kick_recv.at[n_bead - r - 2, p],
                (s, q),
            )
            c.start()
            kick_copies.append(c)

    total = beads * n_bead
    tables = step_tables(total)
    row = lax.broadcasted_iota(jnp.int32, (beads, atoms), 0)

    def column(table, source):
        result = jnp.full((beads, atoms), float(table[(0 - source) % total]), F32)
        for b in range(1, beads):
            result = jnp.where(row == b, float(table[(b - source) % total]), result)
        return result

    for c in peer_copies:
        c.wait_recv()
    kept_pos, moved, kept_mom, pulled = [[0.0] * 3 for _ in range(4)]
    for q in range(n_bead):
        if q == 1:
            for c in kick_copies:
                c.wait_recv()
        for j in range(beads):
            keep, gain, pull = [column(t, q * beads + j) for t in tables]
            for c in range(3):
                if q == 0:
                    where_pos = pos[c, j : j + 1, :]
                    where_kick = kick[j // 2, c, j % 2 : j % 2 + 1, :]
                else:
                    where_pos = peer_pos[q - 1, c, j : j + 1, :]
                    where_kick = peer_kick[q - 1, j // 2, c, j % 2 : j % 2 + 1, :]
                where_pos = jnp.broadcast_to(where_pos, (beads, atoms))
                where_kick = jnp.broadcast_to(where_kick, (beads, atoms))
                kept_pos[c] = kept_pos[c] + where_pos * keep
                moved[c] = moved[c] + where_kick * gain
                kept_mom[c] = kept_mom[c] + where_kick * keep
                pulled[c] = pulled[c] + where_pos * pull
    weight = mass[...]
    inverse = 1.0 / weight
    for c in range(3):
        new_pos[c] = kept_pos[c] + moved[c] * inverse
        new_mom[c] = kept_mom[c] - weight * pulled[c]

    for c in face_copies + pos_copies + peer_copies + kick_copies:
        c.wait_send()
    for both in feat_copies:
        for c in both:
            c.wait_send()


def hand_out(first_in, second_in, first_out, second_out, sems):
    copies = [
        pltpu.make_async_copy(first_in, first_out, sems.at[0]),
        pltpu.make_async_copy(second_in, second_out, sems.at[1]),
    ]
    for c in copies:
        c.start()
    for c in copies:
        c.wait()


def body(
    n_space, n_bead,
    positions, momenta, masses, features, neighbours, images, face_map,
    w_query, w_key, w_value, w_probe, radial_rate,
):
    beads, atoms, channels = features.shape
    heads = radial_rate.shape[0]
    near = neighbours.shape[0]
    terms = 2 * heads
    pairs = beads // 2
    wide = 2 * near
    peers = n_bead - 1
    vmem = pl.BlockSpec(memory_space=pltpu.VMEM)
    hbm = pl.BlockSpec(memory_space=pltpu.HBM)
    dma = pltpu.SemaphoreType.DMA
    shape = jax.ShapeDtypeStruct((3, beads, atoms), F32)
    square = pltpu.VMEM((channels, channels), BF16)
    new_positions, new_momenta = pl.pallas_call(
        functools.partial(step_kernel, n_space, n_bead),
        out_shape=(shape, shape),
        in_specs=[hbm] * 12,
        out_specs=(vmem, vmem),
        scratch_shapes=[
            pltpu.VMEM((3, beads, atoms), F32),
            pltpu.VMEM((3, beads, atoms), F32),
            pltpu.VMEM((1, atoms), F32),
            pltpu.VMEM((beads, atoms, channels), BF16),
            pltpu.VMEM((near, atoms), jnp.int32),
            pltpu.VMEM((near, atoms), jnp.int32),
            square, square, square, square,
            pltpu.SMEM((heads,), F32),
            dma((11,)),
            pltpu.VMEM((beads, 2 * atoms, channels), BF16),
            pltpu.VMEM((2, 3, beads, atoms), F32),
            pltpu.VMEM((2, 1, atoms), jnp.int32),
            pltpu.VMEM((peers, 3, beads, atoms), F32),
            pltpu.VMEM((peers, pairs, 3, 2, atoms), F32),
            pltpu.VMEM((pairs, 3, 2, atoms), F32),
            pltpu.VMEM((beads, terms, atoms, channels), BF16),
            tuple(pltpu.VMEM((terms, atoms, atoms), F32) for _ in range(beads)),
            tuple(pltpu.VMEM((terms, atoms, 2 * atoms), F32) for _ in range(beads)),
            tuple(pltpu.VMEM((terms, atoms, wide), F32) for _ in range(pairs)),
            pltpu.VMEM((atoms, wide), jnp.int32),
            pltpu.VMEM((atoms, wide), jnp.int32),
            pltpu.VMEM((3, atoms, wide), F32),
            pltpu.VMEM((3, atoms, 8), F32),
            pltpu.VMEM((pairs, 3, atoms, wide), F32),
            pltpu.VMEM((heads, atoms, wide), F32),
            pltpu.VMEM((heads, atoms, wide), F32),
            dma((2, beads)), dma((2, beads)), dma((2,)), dma((2,)), dma((2,)), dma((2,)),
            dma((peers,)), dma((peers,)), dma((peers, pairs)), dma((peers, pairs)),
        ],
        compiler_params=pltpu.CompilerParams(
            collective_id=0, has_side_effects=True, vmem_limit_bytes=VMEM_GRANT
        ),
    )(
        positions.transpose(1, 0, 2), momenta.transpose(1, 0, 2), masses.reshape(1, atoms),
        features, neighbours, images, face_map, w_query, w_key, w_value, w_probe, radial_rate,
    )
    new_positions, new_momenta = pl.pallas_call(
        hand_out,
        out_shape=(shape, shape),
        in_specs=[vmem] * 2,
        out_specs=(hbm, hbm),
        scratch_shapes=[dma((2,))],
        compiler_params=pltpu.CompilerParams(vmem_limit_bytes=VMEM_GRANT),
    )(new_positions, new_momenta)
    return new_positions.transpose(1, 0, 2), new_momenta.transpose(1, 0, 2)


def solution(mesh):
    placed = (
        P("bead", None, "space"),
        P("bead", None, "space"),
        P("space"),
        P("bead", "space", None),
        P(None, "space"),
        P(None, "space"),
        P(None, "space", None),
        P(),
        P(),
        P(),
        P(),
        P(),
    )
    return jax.shard_map(
        functools.partial(body, mesh.shape["space"], mesh.shape["bead"]),
        mesh=mesh,
        in_specs=placed,
        out_specs=(P("bead", None, "space"), P("bead", None, "space")),
        check_vma=False,
    )
```
